256 devices in a mesh: seq: 64 (over y, z, core), ch: 4 (over x).
Axes of the slice: x: 4, y: 4, z: 8, core: 2. Of those that a mesh axis runs over, the one named last changes fastest.
Arguments:
- features: bfloat16 [8192, 3, 4096], P('seq', None, 'ch'), may hold values from -6 to 6
- short_weights: float32 [3, 3, 4096], P(None, None, 'ch'), may hold values from -3 to 3
- long_filter: float32 [8192, 4096], P('seq', 'ch'), may hold values from -0.0625 to 0.0625
- skip_gain: float32 [4096], P('ch'), may hold values from -4 to 4
- out_weight: bfloat16 [4096, 4096], P('ch'), may hold values from -0.09375 to 0.09375
Outputs:
- mixed: bfloat16 [8192, 4096], P('seq', 'ch')
The draws below stay inside these ranges and needn't reach their ends.
All inputs are finite; a program needn't handle non-finite values.
Results may differ from the reference program's by a relative error of at most 0.0049.
Values may be sent and summed in bfloat16 or wider, within the bound.
A program may use at most 128 MiB of HBM per device.

```python
import jax
import jax.numpy as jnp

D = 4096
TOKENS = 8192


def steps_of(key, shape, shards, least, top_value):
    def one(position, parts):
        heights = jax.random.uniform(jax.random.fold_in(jax.random.fold_in(key, 6), position), (parts,), jnp.float32, least / len(shards), top_value / len(shards))
        return jnp.repeat(jnp.exp(heights), shape[position] // parts).reshape((-1,) + (1,) * (len(shape) - position - 1))

    level = one(*shards[0])
    for cut in shards[1:]:
        level = level * one(*cut)
    return level


def bell_draw(own_key, extent, width, reach, shards=(), dtype=jnp.bfloat16):
    level = steps_of(own_key, extent, shards, -0.22, 0.18) if shards else 1.0
    drawn = jax.random.normal(own_key, extent, jnp.float32) * width * level
    return jnp.minimum(jnp.maximum(drawn, -reach), reach).astype(dtype)


def setup_inputs(seed: int = 0) -> dict:
    seeds = jax.random.split(jax.random.key(seed), 6)
    features = bell_draw(seeds[0], (TOKENS, 3, D), 1.0, 6.0, ((0, 64), (2, 4)))
    short_weights = bell_draw(seeds[1], (3, 3, D), 0.5, 3.0, ((2, 4),), jnp.float32)
    long_filter = bell_draw(seeds[2], (TOKENS, D), TOKENS ** -0.5, 0.0625, ((0, 64), (1, 4)), jnp.float32)
    skip_gain = bell_draw(seeds[3], (D,), 1.0, 4.0, ((0, 4),), jnp.float32)
    out_weight = bell_draw(seeds[4], (D, D), D ** -0.5, 0.09375, ((0, 4),))
    return dict(features=features, short_weights=short_weights, long_filter=long_filter, skip_gain=skip_gain, out_weight=out_weight)


def reference(features, short_weights, long_filter, skip_gain, out_weight):
    seq_len = features.shape[0]
    widened = features.astype(jnp.float32)
    leading = jnp.zeros((2,) + widened.shape[1:], jnp.float32)
    padded = jnp.concatenate([leading, widened], 0)
    filtered = short_weights[0] * padded[2:] + short_weights[1] * padded[1:-1] + short_weights[2] * padded[:-2]
    query = filtered[:, 0]
    product = filtered[:, 1] * filtered[:, 2]
    spectrum = jnp.fft.rfft(long_filter, n=2 * seq_len, axis=0) * jnp.fft.rfft(product, n=2 * seq_len, axis=0)
    convolved = jnp.fft.irfft(spectrum, n=2 * seq_len, axis=0)[:seq_len].astype(jnp.float32)
    gated = (query * (convolved + skip_gain * product)).astype(jnp.bfloat16)
    return jnp.dot(gated, out_weight, preferred_element_type=jnp.float32).astype(jnp.bfloat16)
```

```python
import numpy as np

import jax
import jax.numpy as jnp
from jax import lax
from jax.sharding import PartitionSpec as P


def tables(blocks, rows):
    seq_len = blocks * rows
    g = np.arange(blocks)[:, None]
    a = np.arange(blocks)[None, :]
    r = np.arange(rows)[None, :]
    outer = np.pi * ((2 * g + 1) * a % (4 * blocks)) / (2 * blocks)
    turn = np.pi * ((2 * g + 1) * r) / (2 * seq_len)
    inner = 2 * np.pi * (np.arange(rows)[:, None] * r % rows) / rows
    as_f32 = lambda x: np.asarray(x, np.float32)
    step_one = as_f32(np.stack([np.cos(outer), -np.sin(outer)]))
    twiddle = as_f32(np.stack([np.cos(turn), np.sin(turn)]))
    cosine, sine = np.cos(inner), np.sin(inner)
    step_two = as_f32(np.block([[cosine, -sine], [sine, cosine]]))
    return step_one, twiddle, step_two


def contract(form, *operands):
    return jnp.einsum(form, *operands, precision=lax.Precision.HIGHEST)


def local(features, short_weights, long_filter, skip_gain, out_weight):
    rows, _, chans = features.shape
    blocks = lax.axis_size("seq")
    own = chans // blocks
    seq_len = rows * blocks
    step_one, twiddle, step_two = tables(blocks, rows)

    def spread(value):
        parts = value.T.astype(jnp.bfloat16).reshape(blocks, own, rows)
        return lax.all_to_all(parts, "seq", 0, 0, tiled=True)

    def forward(parts):
        parts = parts.astype(jnp.float32)
        mixed = contract("pga,acr->pcgr", step_one, parts)
        real = mixed[0] * twiddle[0] + mixed[1] * twiddle[1]
        imag = mixed[1] * twiddle[0] - mixed[0] * twiddle[1]
        out = contract("cgx,xk->cgk", jnp.concatenate([real, imag], -1), step_two)
        return out[..., :rows], out[..., rows:]

    edge = lax.ppermute(features[rows - 2 :], "seq", [(s, s + 1) for s in range(blocks - 1)])
    resp_re, resp_im = forward(spread(long_filter))
    padded = jnp.concatenate([edge, features], 0).astype(jnp.float32)
    filtered = (
        short_weights[0] * padded[2:]
        + short_weights[1] * padded[1:-1]
        + short_weights[2] * padded[:-2]
    )
    query = filtered[:, 0]
    product = filtered[:, 1] * filtered[:, 2]
    sig_re, sig_im = forward(spread(product))
    real = sig_re * resp_re - sig_im * resp_im
    imag = sig_re * resp_im + sig_im * resp_re
    back = contract("cgk,xk->cgx", jnp.concatenate([real, imag], -1), step_two)
    real, imag = back[..., :rows], back[..., rows:]
    turned = jnp.stack(
        [real * twiddle[0] - imag * twiddle[1], imag * twiddle[0] + real * twiddle[1]]
    )
    convolved = contract("pga,pcgr->acr", step_one, turned) / seq_len
    convolved = lax.all_to_all(convolved.astype(jnp.bfloat16), "seq", 0, 0, tiled=True)
    convolved = convolved.reshape(chans, rows).T.astype(jnp.float32)
    gated = (query * (convolved + skip_gain * product)).astype(jnp.bfloat16)
    terms = jnp.dot(gated, out_weight, preferred_element_type=jnp.float32)
    return lax.psum_scatter(terms.astype(jnp.bfloat16), "ch", scatter_dimension=1, tiled=True)


def solution(mesh):
    in_specs = (P("seq", None, "ch"), P(None, None, "ch"), P("seq", "ch"), P("ch"), P("ch", None))
    out_specs = P("seq", "ch")
    return jax.shard_map(local, mesh=mesh, in_specs=in_specs, out_specs=out_specs, check_vma=False)
```

```python
import functools

import numpy as np

import jax
import jax.numpy as jnp
from jax import lax
from jax.experimental import pallas as pl
from jax.experimental.pallas import tpu as pltpu
from jax.sharding import PartitionSpec as P

MESH = pl.DeviceIdType.MESH
BF16 = jnp.bfloat16
F32 = jnp.float32


def halves(table):
    high = np.asarray(table, np.float32).astype(jnp.bfloat16)
    low = (np.asarray(table, np.float64) - high.astype(np.float64)).astype(jnp.bfloat16)
    return high, low


def tables(blocks, rows):
    seq_len = blocks * rows
    g = np.arange(blocks)[:, None]
    a = np.arange(blocks)[None, :]
    r = np.arange(rows)[None, :]
    outer = np.pi * ((2 * g + 1) * a % (4 * blocks)) / (2 * blocks)
    turn = np.pi * ((2 * g + 1) * r) / (2 * seq_len)
    inner = 2 * np.pi * (np.arange(rows)[:, None] * r % rows) / rows
    outer_high, outer_low = halves(np.concatenate([np.cos(outer), -np.sin(outer)], 0))
    back_high, back_low = halves(np.concatenate([np.cos(outer), -np.sin(outer)], 0).T / seq_len)
    cosine, sine = np.cos(inner), np.sin(inner)
    fwd_high, fwd_low = halves(np.block([[cosine, -sine], [sine, cosine]]))
    inv_high, inv_low = halves(np.block([[cosine, sine], [-sine, cosine]]))
    return (
        np.concatenate([outer_high, outer_low], 1),
        np.stack([np.cos(turn), np.sin(turn)]).astype(np.float32),
        np.concatenate([fwd_high, fwd_low], 1).reshape(2 * rows, 4, rows).transpose(1, 0, 2),
        np.concatenate([inv_high, inv_low], 1).reshape(2 * rows, 4, rows).transpose(1, 0, 2),
        np.stack([back_high, back_low]),
    )


def dot(a, b):
    return jnp.dot(a, b, preferred_element_type=F32)


def split(value):
    high = value.astype(BF16)
    return high, (value - high.astype(F32)).astype(BF16)


def dot_split(value, table):
    high, low = split(value)
    first = jnp.concatenate([table[0], table[1]], 1)
    rest = jnp.concatenate([table[2], table[3]], 1)
    return dot(high, first) + dot(low, first) + dot(high, rest)


def kernel(
    dims,
    feat_hbm,
    taps_hbm,
    filt_hbm,
    skip_hbm,
    weight_hbm,
    outer_hbm,
    turn_hbm,
    fwd_hbm,
    inv_hbm,
    back_hbm,
    out_ref,
    feat,
    taps,
    filt,
    skip,
    weight,
    outer,
    turn,
    fwd,
    inv,
    back,
    ext,
    edge_out,
    edge_in,
    query,
    direct,
    filt_out,
    filt_in,
    prod_out,
    prod_in,
    conv_out,
    conv_in,
    stage,
    spectrum,
    gated,
    part,
    part_in,
    load_sem,
    edge_sem,
    send_sem,
    recv_sem,
    part_send,
    part_recv,
):
    blocks, groups, rows, chans = dims
    own = chans // blocks
    me, ch = lax.axis_index("seq"), lax.axis_index("ch")

    barrier = pltpu.get_barrier_semaphore()

    def greet(step, _):
        pl.semaphore_signal(
            barrier, inc=1, device_id=(lax.rem(me + step, blocks), ch), device_id_type=MESH
        )
        return 0

    lax.fori_loop(1, blocks, greet, 0)
    for step in range(1, groups):
        pl.semaphore_signal(
            barrier, inc=1, device_id=(me, lax.rem(ch + step, groups)), device_id_type=MESH
        )

    loads = [
        pltpu.make_async_copy(source, target, load_sem.at[slot])
        for slot, (source, target) in enumerate(
            [
                (filt_hbm, filt),
                (feat_hbm, feat),
                (taps_hbm, taps),
                (skip_hbm, skip),
                (outer_hbm, outer),
                (turn_hbm, turn),
                (fwd_hbm, fwd),
                (inv_hbm, inv),
                (back_hbm, back),
                (weight_hbm, weight),
            ]
        )
    ]
    for load in loads:
        load.start()

    loads[0].wait()
    for j in range(chans // rows):
        lanes = slice(j * rows, (j + 1) * rows)
        filt_out[lanes, :] = filt[:, lanes].T.astype(BF16)
    loads[1].wait()
    edge_out[...] = jnp.zeros_like(edge_out)
    for kind in range(3):
        ext[kind, 8:, :] = feat[kind].astype(F32)
        edge_out[2 * kind : 2 * kind + 2, :] = ext[kind, rows + 6 : rows + 8, :]

    pl.semaphore_wait(barrier, blocks - 1 + groups - 1)

    edge = pltpu.make_async_remote_copy(
        edge_out,
        edge_in,
        edge_sem.at[0],
        edge_sem.at[1],
        device_id=(lax.rem(me + 1, blocks), ch),
        device_id_type=MESH,
    )
    edge.start()

    def spread(source, target, slot):
        def send(step, _):
            peer = lax.rem(me + step, blocks)
            pltpu.make_async_remote_copy(
                source.at[pl.ds(pl.multiple_of(peer * own, own), own)],
                target.at[pl.ds(pl.multiple_of(me * own, own), own)],
                send_sem.at[slot],
                recv_sem.at[slot],
                device_id=(peer, ch),
                device_id_type=MESH,
            ).start()
            return 0

        lax.fori_loop(1, blocks, send, 0)
        mine = pl.ds(pl.multiple_of(me * own, own), own)
        target[mine, :] = source[mine, :]

    def settle(source, target, slot):
        others = pl.ds(0, (blocks - 1) * own)
        copy = pltpu.make_async_copy(source.at[others], target.at[others], recv_sem.at[slot])
        copy.wait()

    def sent(source, target, slot):
        others = pl.ds(0, (blocks - 1) * own)
        copy = pltpu.make_async_copy(source.at[others], target.at[others], send_sem.at[slot])
        copy.wait()

    spread(filt_out, filt_in, 0)

    edge.wait()
    for load in loads[2:]:
        load.wait()
    for kind in range(3):
        ext[kind, 6:8, :] = jnp.where(me == 0, 0.0, edge_in[2 * kind : 2 * kind + 2, :])
    for j in range(chans // rows):
        lanes = slice(j * rows, (j + 1) * rows)
        kinds = [
            taps[0, kind : kind + 1, lanes] * ext[kind, 8 : 8 + rows, lanes]
            + taps[1, kind : kind + 1, lanes] * ext[kind, 7 : 7 + rows, lanes]
            + taps[2, kind : kind + 1, lanes] * ext[kind, 6 : 6 + rows, lanes]
            for kind in range(3)
        ]
        product = kinds[1] * kinds[2]
        query[:, lanes] = kinds[0]
        direct[:, lanes] = skip[:, lanes] * product
        prod_out[lanes, :] = product.T.astype(BF16)

    spread(prod_out, prod_in, 1)

    def forward(source, c):
        pair = jnp.concatenate(
            [source[pl.ds(c + h, blocks, stride=own), :] for h in range(2)], 1
        ).astype(BF16)
        mixed = dot(outer[...], jnp.concatenate([pair, pair], 0))
        turned = []
        for h in range(2):
            lanes = slice(h * rows, (h + 1) * rows)
            real, imag = mixed[:blocks, lanes], mixed[blocks:, lanes]
            turned.append(
                jnp.concatenate(
                    [real * turn[0] + imag * turn[1], imag * turn[0] - real * turn[1]], 1
                )
            )
        return dot_split(jnp.concatenate(turned, 0), fwd)

    settle(filt_out, filt_in, 0)
    stage[...] = filt_in[...].astype(F32)
    for c in range(0, own, 2):
        spectrum[c * blocks : (c + 2) * blocks, :] = forward(stage, c)

    settle(prod_out, prod_in, 1)
    stage[...] = prod_in[...].astype(F32)
    for c in range(0, own, 2):
        signal = forward(stage, c)
        answer = spectrum[c * blocks : (c + 2) * blocks, :]
        sig_re, sig_im = signal[:, :rows], signal[:, rows:]
        ans_re, ans_im = answer[:, :rows], answer[:, rows:]
        both = jnp.concatenate(
            [sig_re * ans_re - sig_im * ans_im, sig_re * ans_im + sig_im * ans_re], 1
        )
        both = dot_split(both, inv)
        turned = []
        for h in range(2):
            real = both[h * blocks : (h + 1) * blocks, :rows]
            imag = both[h * blocks : (h + 1) * blocks, rows:]
            turned.append(
                jnp.concatenate(
                    [real * turn[0] - imag * turn[1], imag * turn[0] + real * turn[1]], 0
                )
            )
        high, low = split(jnp.concatenate(turned, 1))
        result = dot(
            jnp.concatenate([back[0], back[0]], 1), jnp.concatenate([high, low], 0)
        ) + dot(back[1], high)
        for h in range(2):
            stage[pl.ds(c + h, blocks, stride=own), :] = result[:, h * rows : (h + 1) * rows]
    conv_out[...] = stage[...].astype(BF16)

    spread(conv_out, conv_in, 2)
    settle(conv_out, conv_in, 2)
    for j in range(chans // rows):
        lanes = slice(j * rows, (j + 1) * rows)
        convolved = conv_in[lanes, :].astype(F32).T
        gated[:, lanes] = (query[:, lanes] * (convolved + direct[:, lanes])).astype(BF16)

    width = part.shape[2]
    copies = []
    for step in [*range(1, groups), 0]:
        peer = lax.rem(ch + step, groups)
        for n in range(0, width, 256):
            piece = dot(
                gated[...], weight[:, pl.ds(pl.multiple_of(peer * width + n, 128), min(256, width))]
            )
            if step:
                part[step, :, n : n + 256] = piece.astype(BF16)
            else:
                query[:, n : n + 256] = piece
        if step:
            copy = pltpu.make_async_remote_copy(
                part.at[step],
                part_in.at[step],
                part_send.at[step],
                part_recv.at[step],
                device_id=(me, peer),
                device_id_type=MESH,
            )
            copy.start()
            copies.append(copy)
    sent(filt_out, filt_in, 0)
    sent(prod_out, prod_in, 1)
    sent(conv_out, conv_in, 2)
    total = query[:, :width]
    for step, copy in enumerate(copies, 1):
        copy.wait()
        total = total + part_in[step].astype(F32)
    out_ref[...] = total.astype(BF16)


def local(features, short_weights, long_filter, skip_gain, out_weight):
    rows, _, chans = features.shape
    blocks, groups = lax.axis_size("seq"), lax.axis_size("ch")
    width = out_weight.shape[1] // groups
    consts = tables(blocks, rows)
    operands = (
        jnp.transpose(features, (1, 0, 2)),
        short_weights,
        long_filter,
        skip_gain.reshape(1, chans),
        out_weight,
        *consts,
    )
    vmem = pltpu.VMEM
    return pl.pallas_call(
        functools.partial(kernel, (blocks, groups, rows, chans)),
        out_shape=jax.ShapeDtypeStruct((rows, width), BF16),
        in_specs=[pl.BlockSpec(memory_space=pl.ANY)] * len(operands),
        out_specs=pl.BlockSpec(memory_space=pltpu.VMEM),
        scratch_shapes=[
            *[vmem(x.shape, x.dtype) for x in operands],
            vmem((3, rows + 8, chans), F32),
            vmem((8, chans), F32),
            vmem((8, chans), F32),
            vmem((rows, chans), F32),
            vmem((rows, chans), F32),
            *[vmem((chans, rows), BF16)] * 6,
            vmem((chans, rows), F32),
            vmem((chans, 2 * rows), F32),
            vmem((rows, chans), BF16),
            vmem((groups, rows, width), BF16),
            vmem((groups, rows, width), BF16),
            pltpu.SemaphoreType.DMA((len(operands),)),
            pltpu.SemaphoreType.DMA((2,)),
            pltpu.SemaphoreType.DMA((3,)),
            pltpu.SemaphoreType.DMA((3,)),
            pltpu.SemaphoreType.DMA((groups,)),
            pltpu.SemaphoreType.DMA((groups,)),
        ],
        compiler_params=pltpu.CompilerParams(
            collective_id=0, has_side_effects=True, vmem_limit_bytes=62 * 2**20
        ),
        name="convolve_project",
    )(*operands)


def solution(mesh):
    in_specs = (P("seq", None, "ch"), P(None, None, "ch"), P("seq", "ch"), P("ch"), P("ch", None))
    out_specs = P("seq", "ch")
    return jax.shard_map(local, mesh=mesh, in_specs=in_specs, out_specs=out_specs, check_vma=False)
```

```python
import functools

import numpy as np

import jax
import jax.numpy as jnp
from jax import lax
from jax.experimental import pallas as pl
from jax.experimental.pallas import tpu as pltpu
from jax.sharding import PartitionSpec as P

MESH = pl.DeviceIdType.MESH
BF16 = jnp.bfloat16
F32 = jnp.float32


def halves(table):
    high = np.asarray(table, np.float32).astype(jnp.bfloat16)
    low = (np.asarray(table, np.float64) - high.astype(np.float64)).astype(jnp.bfloat16)
    return high, low


def tables(blocks, rows):
    seq_len = blocks * rows
    g = np.arange(blocks)[:, None]
    a = np.arange(blocks)[None, :]
    r = np.arange(rows)[None, :]
    outer = np.pi * ((2 * g + 1) * a % (4 * blocks)) / (2 * blocks)
    turn = np.pi * ((2 * g + 1) * r) / (2 * seq_len)
    inner = 2 * np.pi * (np.arange(rows)[:, None] * r % rows) / rows
    outer_high, outer_low = halves(np.concatenate([np.cos(outer), -np.sin(outer)], 0))
    back_high, back_low = halves(np.concatenate([np.cos(outer), -np.sin(outer)], 0).T / seq_len)
    cosine, sine = np.cos(inner), np.sin(inner)
    fwd_high, fwd_low = halves(np.block([[cosine, -sine], [sine, cosine]]))
    inv_high, inv_low = halves(np.block([[cosine, sine], [-sine, cosine]]))
    return (
        np.concatenate([outer_high, outer_low], 1),
        np.stack([np.cos(turn), np.sin(turn)]).astype(np.float32),
        np.concatenate([fwd_high, fwd_low], 1).reshape(2 * rows, 4, rows).transpose(1, 0, 2),
        np.concatenate([inv_high, inv_low], 1).reshape(2 * rows, 4, rows).transpose(1, 0, 2),
        np.stack([back_high, back_low]),
    )


def dot(a, b):
    return jnp.dot(a, b, preferred_element_type=F32)


def split(value):
    high = value.astype(BF16)
    return high, (value - high.astype(F32)).astype(BF16)


def dot_split(value, table):
    first = jnp.concatenate([table[0], table[1]], 1)
    rest = jnp.concatenate([table[2], table[3]], 1)
    return dot(value, jnp.concatenate([first, first, rest], 0))


def kernel(
    dims,
    feat_hbm,
    taps_hbm,
    filt_hbm,
    skip_hbm,
    weight_hbm,
    outer_hbm,
    turn_hbm,
    fwd_hbm,
    inv_hbm,
    back_hbm,
    out_ref,
    feat,
    taps,
    filt,
    skip,
    weight,
    outer,
    turn,
    fwd,
    inv,
    back,
    ext,
    edge_out,
    edge_in,
    query,
    direct,
    filt_out,
    filt_in,
    prod_out,
    prod_in,
    conv_out,
    conv_in,
    stage,
    spectrum,
    signal,
    pieces,
    total,
    gated,
    part,
    part_in,
    load_sem,
    edge_sem,
    send_sem,
    recv_sem,
    part_send,
    part_recv,
):
    blocks, groups, rows, chans = dims
    own = chans // blocks
    me, ch = lax.axis_index("seq"), lax.axis_index("ch")

    barrier = pltpu.get_barrier_semaphore()

    def greet(step, _):
        pl.semaphore_signal(
            barrier, inc=1, device_id=(lax.rem(me + step, blocks), ch), device_id_type=MESH
        )
        return 0

    lax.fori_loop(1, blocks, greet, 0)
    for step in range(1, groups):
        pl.semaphore_signal(
            barrier, inc=1, device_id=(me, lax.rem(ch + step, groups)), device_id_type=MESH
        )

    loads = [
        pltpu.make_async_copy(source, target, load_sem.at[slot])
        for slot, (source, target) in enumerate(
            [
                (filt_hbm, filt),
                (feat_hbm, feat),
                (taps_hbm, taps),
                (skip_hbm, skip),
                (outer_hbm, outer),
                (turn_hbm, turn),
                (fwd_hbm, fwd),
                (inv_hbm, inv),
                (back_hbm, back),
                (weight_hbm, weight),
            ]
        )
    ]
    for load in loads:
        load.start()

    loads[0].wait()
    half = chans // 2
    count = rows // (own // 2)
    for j in range(half // rows):
        both = [
            filt[:, g * half + j * rows : g * half + (j + 1) * rows].T.reshape(count, own // 2, rows)
            for g in range(2)
        ]
        filt_out[j * count : (j + 1) * count] = jnp.concatenate(both, 1).astype(BF16)
    loads[1].wait()
    edge_out[...] = jnp.zeros_like(edge_out)
    for kind in range(3):
        ext[kind, 8:, :] = feat[kind].astype(F32)
        edge_out[2 * kind : 2 * kind + 2, :] = ext[kind, rows + 6 : rows + 8, :]

    pl.semaphore_wait(barrier, blocks - 1 + groups - 1)

    edge = pltpu.make_async_remote_copy(
        edge_out,
        edge_in,
        edge_sem.at[0],
        edge_sem.at[1],
        device_id=(lax.rem(me + 1, blocks), ch),
        device_id_type=MESH,
    )
    edge.start()

    my_y, my_z, my_core = me // 16, lax.rem(me // 2, 8), lax.rem(me, 2)

    def spread(source, target, slot):
        def send(dy, dz, core):
            peer = (lax.rem(my_y + dy, 4) * 8 + lax.rem(my_z + dz, 8)) * 2 + core
            pltpu.make_async_remote_copy(
                source.at[peer],
                target.at[me],
                send_sem.at[slot],
                recv_sem.at[slot],
                device_id=(peer, ch),
                device_id_type=MESH,
            ).start()

        def plane(dz, step, _):
            send(lax.rem(step // 2 + 2, 4), dz, lax.rem(step, 2))
            return 0

        for dz in (4, 3, 5, 2, 6, 1, 7):
            lax.fori_loop(0, 8, functools.partial(plane, dz), 0)
        for dy in (2, 3, 1):
            for core in range(2):
                send(dy, 0, core)
        send(0, 0, 1 - my_core)
        target[me] = source[me]

    def settle(source, target, slot):
        others = pl.ds(0, blocks - 1)
        copy = pltpu.make_async_copy(source.at[others], target.at[others], recv_sem.at[slot])
        copy.wait()

    def sent(source, target, slot):
        others = pl.ds(0, blocks - 1)
        copy = pltpu.make_async_copy(source.at[others], target.at[others], send_sem.at[slot])
        copy.wait()

    spread(filt_out, filt_in, 0)

    edge.wait()
    for load in loads[2:]:
        load.wait()
    for kind in range(3):
        ext[kind, 6:8, :] = jnp.where(me == 0, 0.0, edge_in[2 * kind : 2 * kind + 2, :])
    for g in range(2):
        for j in range(half // rows):
            lanes = slice(g * half + j * rows, g * half + (j + 1) * rows)
            kinds = [
                taps[0, kind : kind + 1, lanes] * ext[kind, 8 : 8 + rows, lanes]
                + taps[1, kind : kind + 1, lanes] * ext[kind, 7 : 7 + rows, lanes]
                + taps[2, kind : kind + 1, lanes] * ext[kind, 6 : 6 + rows, lanes]
                for kind in range(3)
            ]
            product = kinds[1] * kinds[2]
            query[:, lanes] = kinds[0]
            direct[:, lanes] = skip[:, lanes] * product
            block = product.T.reshape(count, own // 2, rows)
            prod_out[g, j * count : (j + 1) * count] = block.astype(BF16)
        spread(prod_out.at[g], prod_in.at[g], 1 + g)

    def forward(number):
        for c in range(0, number, 2):
            pair = jnp.concatenate(
                [stage[pl.ds(c + h, blocks, stride=number), :] for h in range(2)], 1
            ).astype(BF16)
            mixed = dot(outer[...], jnp.concatenate([pair, pair], 0))
            for h in range(2):
                lanes = slice(h * rows, (h + 1) * rows)
                real, imag = mixed[:blocks, lanes], mixed[blocks:, lanes]
                keep(
                    (c + h) * blocks,
                    jnp.concatenate(
                        [real * turn[0] + imag * turn[1], imag * turn[0] - real * turn[1]], 1
                    ),
                )

    def keep(start, value):
        high, low = split(value)
        pieces[start : start + blocks, : 2 * rows] = high
        pieces[start : start + blocks, 2 * rows : 4 * rows] = low
        pieces[start : start + blocks, 4 * rows :] = high

    settle(filt_out, filt_in, 0)
    stage[...] = filt_in[...].astype(F32).reshape(chans, rows)
    forward(own)
    spectrum[...] = dot_split(pieces[...], fwd)

    for g in range(2):
        settle(prod_out.at[g], prod_in.at[g], 1 + g)
        stage[:half] = prod_in[g].astype(F32).reshape(half, rows)
        forward(own // 2)
        signal[...] = dot_split(pieces[:half], fwd)
        for start in range(0, half, blocks):
            here = slice(start, start + blocks)
            there = slice(g * half + start, g * half + start + blocks)
            sig_re, sig_im = signal[here, :rows], signal[here, rows:]
            ans_re, ans_im = spectrum[there, :rows], spectrum[there, rows:]
            keep(
                start,
                jnp.concatenate(
                    [sig_re * ans_re - sig_im * ans_im, sig_re * ans_im + sig_im * ans_re], 1
                ),
            )
        signal[...] = dot_split(pieces[:half], inv)
        for c in range(0, own // 2, 2):
            turned = []
            for h in range(2):
                here = slice((c + h) * blocks, (c + h + 1) * blocks)
                real, imag = signal[here, :rows], signal[here, rows:]
                turned.append(
                    jnp.concatenate(
                        [real * turn[0] - imag * turn[1], imag * turn[0] + real * turn[1]], 0
                    )
                )
            high, low = split(jnp.concatenate(turned, 1))
            result = dot(
                jnp.concatenate([back[0], back[0], back[1]], 1),
                jnp.concatenate([high, low, high], 0),
            )
            for h in range(2):
                stage[pl.ds(c + h, blocks, stride=own // 2), :] = result[
                    :, h * rows : (h + 1) * rows
                ]
        conv_out[g] = stage[:half].reshape(blocks, own // 2, rows).astype(BF16)
        spread(conv_out.at[g], conv_in.at[g], 3 + g)

    wide = part.shape[2]
    right, left = lax.rem(ch + 1, 4), lax.rem(ch + 3, 4)
    far = lax.rem(ch + 2, 4)
    plan = [(far, 0), (far, 1), (right, 1), (left, 0), (right, 0), (left, 1), (ch, 0), (ch, 1)]

    def pass_on(slot):
        copy = pltpu.make_async_remote_copy(
            part.at[slot],
            part_in.at[slot],
            part_send.at[slot],
            part_recv.at[slot],
            device_id=(me, left if slot % 2 else right),
            device_id_type=MESH,
        )
        copy.start()
        return copy

    def project(g, slot):
        owner, side = plan[slot]
        start = pl.multiple_of(owner * 2 * wide + side * wide, 128)
        return dot(
            gated[:, g * half : (g + 1) * half],
            weight[g * half : (g + 1) * half, pl.ds(start, wide)],
        )

    copies = []
    for g in range(2):
        settle(conv_out.at[g], conv_in.at[g], 3 + g)
        for j in range(half // rows):
            lanes = slice(g * half + j * rows, g * half + (j + 1) * rows)
            block = conv_in[g, j * count : (j + 1) * count].astype(F32).reshape(rows, rows)
            gated[:, lanes] = (query[:, lanes] * (block.T + direct[:, lanes])).astype(BF16)

        if g == 0:
            for slot in range(8):
                total[slot] = project(0, slot)
            continue
        for slot in range(8):
            piece = total[slot] + project(1, slot)
            if slot in (4, 5):
                copies[slot - 4].wait()
                piece = piece + part_in[slot - 4].astype(F32)
            if slot < 6:
                part[slot] = piece.astype(BF16)
                copies.append(pass_on(slot))
            else:
                total[slot] = piece
    sent(filt_out, filt_in, 0)
    for g in range(2):
        sent(prod_out.at[g], prod_in.at[g], 1 + g)
        sent(conv_out.at[g], conv_in.at[g], 3 + g)
    for copy in copies[2:]:
        copy.wait()
    for side, slots in enumerate([(3, 4), (2, 5)]):
        piece = total[6 + side]
        for slot in slots:
            piece = piece + part_in[slot].astype(F32)
        out_ref[:, side * wide : (side + 1) * wide] = piece.astype(BF16)


def local(features, short_weights, long_filter, skip_gain, out_weight):
    rows, _, chans = features.shape
    blocks, groups = lax.axis_size("seq"), lax.axis_size("ch")
    width = out_weight.shape[1] // groups
    consts = tables(blocks, rows)
    operands = (
        jnp.transpose(features, (1, 0, 2)),
        short_weights,
        long_filter,
        skip_gain.reshape(1, chans),
        out_weight,
        *consts,
    )
    vmem = pltpu.VMEM
    return pl.pallas_call(
        functools.partial(kernel, (blocks, groups, rows, chans)),
        out_shape=jax.ShapeDtypeStruct((rows, width), BF16),
        in_specs=[pl.BlockSpec(memory_space=pl.ANY)] * len(operands),
        out_specs=pl.BlockSpec(memory_space=pltpu.VMEM),
        scratch_shapes=[
            *[vmem(x.shape, x.dtype) for x in operands],
            vmem((3, rows + 8, chans), F32),
            vmem((8, chans), F32),
            vmem((8, chans), F32),
            vmem((rows, chans), F32),
            vmem((rows, chans), F32),
            *[vmem((blocks, chans // blocks, rows), BF16)] * 2,
            *[vmem((2, blocks, chans // blocks // 2, rows), BF16)] * 4,
            vmem((chans, rows), F32),
            vmem((chans, 2 * rows), F32),
            vmem((chans // 2, 2 * rows), F32),
            vmem((chans, 6 * rows), BF16),
            vmem((8, rows, width // 2), F32),
            vmem((rows, chans), BF16),
            vmem((6, rows, width // 2), BF16),
            vmem((6, rows, width // 2), BF16),
            pltpu.SemaphoreType.DMA((len(operands),)),
            pltpu.SemaphoreType.DMA((2,)),
            pltpu.SemaphoreType.DMA((5,)),
            pltpu.SemaphoreType.DMA((5,)),
            pltpu.SemaphoreType.DMA((6,)),
            pltpu.SemaphoreType.DMA((6,)),
        ],
        compiler_params=pltpu.CompilerParams(
            collective_id=0, has_side_effects=True, vmem_limit_bytes=62 * 2**20
        ),
        name="convolve_project",
    )(*operands)


def solution(mesh):
    in_specs = (P("seq", None, "ch"), P(None, None, "ch"), P("seq", "ch"), P("ch"), P("ch", None))
    out_specs = P("seq", "ch")
    return jax.shard_map(local, mesh=mesh, in_specs=in_specs, out_specs=out_specs, check_vma=False)
```

```python
import functools

import numpy as np

import jax
import jax.numpy as jnp
from jax import lax
from jax.experimental import pallas as pl
from jax.experimental.pallas import tpu as pltpu
from jax.sharding import PartitionSpec as P

MESH = pl.DeviceIdType.MESH
PARTS = 2
GROUPS = 2
STAGED = (False, False, True)
BF16 = jnp.bfloat16
F32 = jnp.float32


def halves(table):
    high = np.asarray(table, np.float32).astype(jnp.bfloat16)
    low = (np.asarray(table, np.float64) - high.astype(np.float64)).astype(jnp.bfloat16)
    return high, low


def tables(blocks, rows):
    seq_len = blocks * rows
    g = np.arange(blocks)[:, None]
    a = np.arange(blocks)[None, :]
    r = np.arange(rows)[None, :]
    outer = np.pi * ((2 * g + 1) * a % (4 * blocks)) / (2 * blocks)
    turn = np.pi * ((2 * g + 1) * r) / (2 * seq_len)
    inner = 2 * np.pi * (np.arange(rows)[:, None] * r % rows) / rows
    outer_high, outer_low = halves(np.concatenate([np.cos(outer), -np.sin(outer)], 0))
    back_high, back_low = halves(np.concatenate([np.cos(outer), -np.sin(outer)], 0).T / seq_len)
    cosine, sine = np.cos(inner), np.sin(inner)
    fwd_high, fwd_low = halves(np.block([[cosine, -sine], [sine, cosine]]))
    inv_high, inv_low = halves(np.block([[cosine, sine], [-sine, cosine]]))
    return (
        np.concatenate([outer_high, outer_low], 1),
        np.stack([np.cos(turn), np.sin(turn)]).astype(np.float32),
        np.concatenate([fwd_high, fwd_low], 1).reshape(2 * rows, 4, rows).transpose(1, 0, 2),
        np.concatenate([inv_high, inv_low], 1).reshape(2 * rows, 4, rows).transpose(1, 0, 2),
        np.stack([back_high, back_low]),
    )


def dot(a, b):
    return jnp.dot(a, b, preferred_element_type=F32)


def split(value):
    high = value.astype(BF16)
    return high, (value - high.astype(F32)).astype(BF16)


def dot_split(value, table):
    first = jnp.concatenate([table[0], table[1]], 1)
    rest = jnp.concatenate([table[2], table[3]], 1)
    return dot(value, jnp.concatenate([first, first, rest], 0))


def order(staged):
    def distance(step):
        dy, dz, core = step
        return (1 - core if staged else 0, -min(dy, 4 - dy) - min(dz, 8 - dz), -min(dz, 8 - dz))

    steps = [(dy, dz, core) for dy in range(4) for dz in range(8) for core in range(2) if dy or dz]
    return sorted(steps, key=distance)


def kernel(
    dims,
    feat_hbm,
    taps_hbm,
    filt_hbm,
    skip_hbm,
    weight_hbm,
    outer_hbm,
    turn_hbm,
    fwd_hbm,
    inv_hbm,
    back_hbm,
    out_ref,
    feat,
    taps,
    filt,
    skip,
    weight,
    outer,
    turn,
    fwd,
    inv,
    back,
    ext,
    edge_out,
    edge_in,
    query,
    direct,
    filt_out,
    filt_in,
    prod_out,
    prod_in,
    conv_out,
    conv_in,
    stage,
    spectrum,
    signal,
    pieces,
    total,
    gated,
    part,
    part_in,
    load_sem,
    edge_sem,
    send_sem,
    recv_sem,
    part_send,
    part_recv,
):
    blocks, groups, rows, chans = dims
    own = chans // blocks
    me, ch = lax.axis_index("seq"), lax.axis_index("ch")

    my_y, my_z, my_core = me // 16, lax.rem(me // 2, 8), lax.rem(me, 2)
    along_y = [lax.rem(my_y + dy, 4) * 16 for dy in range(4)]
    along_z = [lax.rem(my_z + dz, 8) * 2 for dz in range(8)]

    barrier = pltpu.get_barrier_semaphore()

    def greet(peer):
        pl.semaphore_signal(barrier, inc=1, device_id=(peer, ch), device_id_type=MESH)

    for dy, dz, core in order(False):
        greet(along_y[dy] + along_z[dz] + core)
    greet(along_y[0] + along_z[0] + 1 - my_core)
    for step in range(1, groups):
        pl.semaphore_signal(
            barrier, inc=1, device_id=(me, lax.rem(ch + step, groups)), device_id_type=MESH
        )

    loads = [
        pltpu.make_async_copy(source, target, load_sem.at[slot])
        for slot, (source, target) in enumerate(
            [
                (filt_hbm, filt),
                (feat_hbm, feat),
                (taps_hbm, taps),
                (skip_hbm, skip),
                (outer_hbm, outer),
                (turn_hbm, turn),
                (fwd_hbm, fwd),
                (inv_hbm, inv),
                (back_hbm, back),
                (weight_hbm, weight),
            ]
        )
    ]
    for load in loads:
        load.start()

    loads[0].wait()
    each = own // GROUPS
    half = chans // GROUPS
    count = rows // each
    for g in range(GROUPS):
        for j in range(half // rows):
            block = filt[:, g * half + j * rows : g * half + (j + 1) * rows].T
            filt_out[g, j * count : (j + 1) * count] = block.reshape(count, each, rows).astype(BF16)
    loads[1].wait()
    edge_out[...] = jnp.zeros_like(edge_out)
    for kind in range(3):
        ext[kind, 8:, :] = feat[kind].astype(F32)
        edge_out[2 * kind : 2 * kind + 2, :] = ext[kind, rows + 6 : rows + 8, :]

    pl.semaphore_wait(barrier, blocks - 1 + groups - 1)

    edge = pltpu.make_async_remote_copy(
        edge_out,
        edge_in,
        edge_sem.at[0],
        edge_sem.at[1],
        device_id=(lax.rem(me + 1, blocks), ch),
        device_id_type=MESH,
    )
    edge.start()

    def spread(source, target, slot, staged=False):
        def send(dy, dz, core):
            peer = along_y[dy] + along_z[dz] + core
            pltpu.make_async_remote_copy(
                source.at[peer],
                target.at[me],
                send_sem.at[slot],
                recv_sem.at[slot],
                device_id=(peer, ch),
                device_id_type=MESH,
            ).start()

        for dy, dz, core in order(staged):
            send(dy, dz, core)
        send(0, 0, 1 - my_core)
        target[me] = source[me]

    def settle(source, target, slot):
        others = pl.ds(0, blocks - 1)
        copy = pltpu.make_async_copy(source.at[others], target.at[others], recv_sem.at[slot])
        copy.wait()

    def sent(source, target, slot):
        others = pl.ds(0, blocks - 1)
        copy = pltpu.make_async_copy(source.at[others], target.at[others], send_sem.at[slot])
        copy.wait()

    for g in range(GROUPS):
        spread(filt_out.at[g], filt_in.at[g], g, STAGED[0])
        if g == 0:
            edge.wait()
            for load in loads[2:4]:
                load.wait()
            for kind in range(3):
                ext[kind, 6:8, :] = jnp.where(me == 0, 0.0, edge_in[2 * kind : 2 * kind + 2, :])
        for j in range(half // rows):
            lanes = slice(g * half + j * rows, g * half + (j + 1) * rows)
            kinds = [
                taps[0, kind : kind + 1, lanes] * ext[kind, 8 : 8 + rows, lanes]
                + taps[1, kind : kind + 1, lanes] * ext[kind, 7 : 7 + rows, lanes]
                + taps[2, kind : kind + 1, lanes] * ext[kind, 6 : 6 + rows, lanes]
                for kind in range(3)
            ]
            product = kinds[1] * kinds[2]
            query[:, lanes] = kinds[0]
            direct[:, lanes] = skip[:, lanes] * product
            block = product.T.reshape(count, each, rows)
            prod_out[g, j * count : (j + 1) * count] = block.astype(BF16)
        spread(prod_out.at[g], prod_in.at[g], GROUPS + g, STAGED[1])
    for load in loads[4:]:
        load.wait()

    def forward(number):
        for c in range(0, number, 2):
            pair = jnp.concatenate(
                [stage[pl.ds(c + h, blocks, stride=number), :] for h in range(2)], 1
            ).astype(BF16)
            mixed = dot(outer[...], jnp.concatenate([pair, pair], 0))
            for h in range(2):
                lanes = slice(h * rows, (h + 1) * rows)
                real, imag = mixed[:blocks, lanes], mixed[blocks:, lanes]
                keep(
                    (c + h) * blocks,
                    jnp.concatenate(
                        [real * turn[0] + imag * turn[1], imag * turn[0] - real * turn[1]], 1
                    ),
                )

    def keep(start, value):
        high, low = split(value)
        pieces[start : start + blocks, : 2 * rows] = high
        pieces[start : start + blocks, 2 * rows : 4 * rows] = low
        pieces[start : start + blocks, 4 * rows :] = high

    for g in range(GROUPS):
        settle(filt_out.at[g], filt_in.at[g], g)
        stage[...] = filt_in[g].astype(F32).reshape(half, rows)
        forward(each)
        spectrum[...] = dot_split(pieces[...], fwd)
        settle(prod_out.at[g], prod_in.at[g], GROUPS + g)
        stage[...] = prod_in[g].astype(F32).reshape(half, rows)
        forward(each)
        signal[...] = dot_split(pieces[...], fwd)
        for start in range(0, half, blocks):
            here = slice(start, start + blocks)
            sig_re, sig_im = signal[here, :rows], signal[here, rows:]
            ans_re, ans_im = spectrum[here, :rows], spectrum[here, rows:]
            keep(
                start,
                jnp.concatenate(
                    [sig_re * ans_re - sig_im * ans_im, sig_re * ans_im + sig_im * ans_re], 1
                ),
            )
        signal[...] = dot_split(pieces[...], inv)
        for c in range(0, each, 2):
            turned = []
            for h in range(2):
                here = slice((c + h) * blocks, (c + h + 1) * blocks)
                real, imag = signal[here, :rows], signal[here, rows:]
                turned.append(
                    jnp.concatenate(
                        [real * turn[0] - imag * turn[1], imag * turn[0] + real * turn[1]], 0
                    )
                )
            high, low = split(jnp.concatenate(turned, 1))
            result = dot(
                jnp.concatenate([back[0], back[0], back[1]], 1),
                jnp.concatenate([high, low, high], 0),
            )
            for h in range(2):
                stage[pl.ds(c + h, blocks, stride=each), :] = result[
                    :, h * rows : (h + 1) * rows
                ]
        conv_out[g] = stage[...].reshape(blocks, each, rows).astype(BF16)
        spread(conv_out.at[g], conv_in.at[g], 2 * GROUPS + g, STAGED[2])

    fine = part.shape[3]
    wide = PARTS * fine
    right, left = lax.rem(ch + 1, 4), lax.rem(ch + 3, 4)
    far = lax.rem(ch + 2, 4)
    plan = [(far, 0), (far, 1), (right, 1), (left, 0), (right, 0), (left, 1), (ch, 0), (ch, 1)]

    def pass_on(slot, n):
        copy = pltpu.make_async_remote_copy(
            part.at[slot, n],
            part_in.at[slot, n],
            part_send.at[slot, n],
            part_recv.at[slot, n],
            device_id=(me, left if slot % 2 else right),
            device_id_type=MESH,
        )
        copy.start()
        return copy

    def project(g, slot):
        owner, side = plan[slot]
        start = pl.multiple_of(owner * 2 * wide + side * wide, 128)
        return dot(
            gated[:, g * half : (g + 1) * half],
            weight[g * half : (g + 1) * half, pl.ds(start, wide)],
        )

    copies = {}
    for g in range(GROUPS):
        settle(conv_out.at[g], conv_in.at[g], 2 * GROUPS + g)
        for j in range(half // rows):
            lanes = slice(g * half + j * rows, g * half + (j + 1) * rows)
            block = conv_in[g, j * count : (j + 1) * count].astype(F32).reshape(rows, rows)
            gated[:, lanes] = (query[:, lanes] * (block.T + direct[:, lanes])).astype(BF16)

        for slot in range(8):
            piece = project(g, slot) if g == 0 else total[slot] + project(g, slot)
            if g < GROUPS - 1:
                total[slot] = piece
                continue
            if slot < 4:
                for n in range(PARTS):
                    part[slot, n] = piece[:, n * fine : (n + 1) * fine].astype(BF16)
                    copies[slot, n] = pass_on(slot, n)
            else:
                total[slot] = piece
    for n in range(PARTS):
        for slot in (4, 5):
            copies[slot - 4, n].wait()
            piece = total[slot, :, n * fine : (n + 1) * fine]
            part[slot, n] = (piece + part_in[slot - 4, n].astype(F32)).astype(BF16)
            copies[slot, n] = pass_on(slot, n)
    for g in range(GROUPS):
        sent(filt_out.at[g], filt_in.at[g], g)
        sent(prod_out.at[g], prod_in.at[g], GROUPS + g)
        sent(conv_out.at[g], conv_in.at[g], 2 * GROUPS + g)
    for slot in (2, 3):
        for n in range(PARTS):
            copies[slot, n].wait()
    for n in range(PARTS):
        for side, slots in enumerate([(3, 4), (2, 5)]):
            copies[4 + side, n].wait()
        for side, slots in enumerate([(3, 4), (2, 5)]):
            piece = total[6 + side, :, n * fine : (n + 1) * fine]
            for slot in slots:
                piece = piece + part_in[slot, n].astype(F32)
            out_ref[:, side * wide + n * fine : side * wide + (n + 1) * fine] = piece.astype(BF16)


def local(features, short_weights, long_filter, skip_gain, out_weight):
    rows, _, chans = features.shape
    blocks, groups = lax.axis_size("seq"), lax.axis_size("ch")
    width = out_weight.shape[1] // groups
    consts = tables(blocks, rows)
    operands = (
        jnp.transpose(features, (1, 0, 2)),
        short_weights,
        long_filter,
        skip_gain.reshape(1, chans),
        out_weight,
        *consts,
    )
    vmem = pltpu.VMEM
    return pl.pallas_call(
        functools.partial(kernel, (blocks, groups, rows, chans)),
        out_shape=pltpu.VMEM((rows, width), BF16),
        in_specs=[pl.BlockSpec(memory_space=pl.ANY)] * len(operands),
        out_specs=pl.BlockSpec(memory_space=pltpu.VMEM),
        scratch_shapes=[
            *[vmem(x.shape, x.dtype) for x in operands],
            vmem((3, rows + 8, chans), F32),
            vmem((8, chans), F32),
            vmem((8, chans), F32),
            vmem((rows, chans), F32),
            vmem((rows, chans), F32),
            *[vmem((GROUPS, blocks, chans // blocks // GROUPS, rows), BF16)] * 6,
            vmem((chans // GROUPS, rows), F32),
            vmem((chans // GROUPS, 2 * rows), F32),
            vmem((chans // GROUPS, 2 * rows), F32),
            vmem((chans // GROUPS, 6 * rows), BF16),
            vmem((8, rows, width // 2), F32),
            vmem((rows, chans), BF16),
            vmem((6, PARTS, rows, width // 2 // PARTS), BF16),
            vmem((6, PARTS, rows, width // 2 // PARTS), BF16),
            pltpu.SemaphoreType.DMA((len(operands),)),
            pltpu.SemaphoreType.DMA((2,)),
            pltpu.SemaphoreType.DMA((3 * GROUPS,)),
            pltpu.SemaphoreType.DMA((3 * GROUPS,)),
            pltpu.SemaphoreType.DMA((6, PARTS)),
            pltpu.SemaphoreType.DMA((6, PARTS)),
        ],
        compiler_params=pltpu.CompilerParams(
            collective_id=0, has_side_effects=True, vmem_limit_bytes=62 * 2**20
        ),
        name="convolve_project",
    )(*operands)


def solution(mesh):
    in_specs = (P("seq", None, "ch"), P(None, None, "ch"), P("seq", "ch"), P("ch"), P("ch", None))
    out_specs = P("seq", "ch")
    return jax.shard_map(local, mesh=mesh, in_specs=in_specs, out_specs=out_specs, check_vma=False)
```

```python
import functools

import numpy as np

import jax
import jax.numpy as jnp
from jax import lax
from jax.experimental import pallas as pl
from jax.experimental.pallas import tpu as pltpu
from jax.sharding import PartitionSpec as P

MESH = pl.DeviceIdType.MESH
PARTS = 2
GROUPS = 2
STAGED = (False, False, True)
BF16 = jnp.bfloat16
F32 = jnp.float32


def halves(table):
    high = np.asarray(table, np.float32).astype(jnp.bfloat16)
    low = (np.asarray(table, np.float64) - high.astype(np.float64)).astype(jnp.bfloat16)
    return high, low


def tables(blocks, rows):
    seq_len = blocks * rows
    g = np.arange(blocks)[:, None]
    a = np.arange(blocks)[None, :]
    r = np.arange(rows)[None, :]
    outer = np.pi * ((2 * g + 1) * a % (4 * blocks)) / (2 * blocks)
    turn = np.pi * ((2 * g + 1) * r) / (2 * seq_len)
    inner = 2 * np.pi * (np.arange(rows)[:, None] * r % rows) / rows
    outer_high, outer_low = halves(np.concatenate([np.cos(outer), -np.sin(outer)], 0))
    back_high, back_low = halves(np.concatenate([np.cos(outer), -np.sin(outer)], 0).T / seq_len)
    cosine, sine = np.cos(inner), np.sin(inner)
    fwd_high, fwd_low = halves(np.block([[cosine, -sine], [sine, cosine]]))
    inv_high, inv_low = halves(np.block([[cosine, sine], [-sine, cosine]]))
    return (
        np.concatenate([outer_high, outer_low], 1),
        np.stack([np.cos(turn), np.sin(turn)]).astype(np.float32),
        np.concatenate([fwd_high, fwd_low], 1).reshape(2 * rows, 4, rows).transpose(1, 0, 2),
        np.concatenate([inv_high, inv_low], 1).reshape(2 * rows, 4, rows).transpose(1, 0, 2),
        np.stack([back_high, back_low]),
    )


def dot(a, b):
    return jnp.dot(a, b, preferred_element_type=F32)


def split(value):
    high = value.astype(BF16)
    return high, (value - high.astype(F32)).astype(BF16)


def dot_split(value, table):
    first = jnp.concatenate([table[0], table[1]], 1)
    rest = jnp.concatenate([table[2], table[3]], 1)
    return dot(value, jnp.concatenate([first, first, rest], 0))


def order(staged):
    def distance(step):
        dy, dz, core = step
        return (1 - core if staged else 0, -min(dy, 4 - dy) - min(dz, 8 - dz), (dy + dz) % 2, dz)

    steps = [(dy, dz, core) for dy in range(4) for dz in range(8) for core in range(2) if dy or dz]
    return sorted(steps, key=distance)


def kernel(
    dims,
    feat_hbm,
    taps_hbm,
    filt_hbm,
    skip_hbm,
    weight_hbm,
    outer_hbm,
    turn_hbm,
    fwd_hbm,
    inv_hbm,
    back_hbm,
    out_ref,
    feat,
    taps,
    filt,
    skip,
    weight,
    outer,
    turn,
    fwd,
    inv,
    back,
    ext,
    edge_out,
    edge_in,
    query,
    direct,
    filt_out,
    filt_in,
    prod_out,
    prod_in,
    conv_out,
    conv_in,
    stage,
    spectrum,
    signal,
    pieces,
    total,
    gated,
    part,
    part_in,
    load_sem,
    edge_sem,
    send_sem,
    recv_sem,
    part_send,
    part_recv,
):
    blocks, groups, rows, chans = dims
    own = chans // blocks
    me, ch = lax.axis_index("seq"), lax.axis_index("ch")

    my_y, my_z, my_core = me // 16, lax.rem(me // 2, 8), lax.rem(me, 2)
    along_y = [lax.rem(my_y + dy, 4) * 16 for dy in range(4)]
    along_z = [lax.rem(my_z + dz, 8) * 2 for dz in range(8)]

    barrier = pltpu.get_barrier_semaphore()

    def greet(peer):
        pl.semaphore_signal(barrier, inc=1, device_id=(peer, ch), device_id_type=MESH)

    for dy, dz, core in order(False):
        greet(along_y[dy] + along_z[dz] + core)
    greet(along_y[0] + along_z[0] + 1 - my_core)
    for step in range(1, groups):
        pl.semaphore_signal(
            barrier, inc=1, device_id=(me, lax.rem(ch + step, groups)), device_id_type=MESH
        )

    loads = [
        pltpu.make_async_copy(source, target, load_sem.at[slot])
        for slot, (source, target) in enumerate(
            [
                (filt_hbm, filt),
                (feat_hbm, feat),
                (taps_hbm, taps),
                (skip_hbm, skip),
                (outer_hbm, outer),
                (turn_hbm, turn),
                (fwd_hbm, fwd),
                (inv_hbm, inv),
                (back_hbm, back),
                (weight_hbm, weight),
            ]
        )
    ]
    for load in loads:
        load.start()

    loads[0].wait()
    each = own // GROUPS
    half = chans // GROUPS
    count = rows // each
    for g in range(GROUPS):
        for j in range(half // rows):
            block = filt[:, g * half + j * rows : g * half + (j + 1) * rows].T
            filt_out[g, j * count : (j + 1) * count] = block.reshape(count, each, rows).astype(BF16)
    loads[1].wait()
    edge_out[...] = jnp.zeros_like(edge_out)
    for kind in range(3):
        ext[kind, 8:, :] = feat[kind].astype(F32)
        edge_out[2 * kind : 2 * kind + 2, :] = ext[kind, rows + 6 : rows + 8, :]

    pl.semaphore_wait(barrier, blocks - 1 + groups - 1)

    edge = pltpu.make_async_remote_copy(
        edge_out,
        edge_in,
        edge_sem.at[0],
        edge_sem.at[1],
        device_id=(lax.rem(me + 1, blocks), ch),
        device_id_type=MESH,
    )
    edge.start()

    def spread(source, target, slot, staged=False):
        def send(dy, dz, core):
            peer = along_y[dy] + along_z[dz] + core
            pltpu.make_async_remote_copy(
                source.at[peer],
                target.at[me],
                send_sem.at[slot],
                recv_sem.at[slot],
                device_id=(peer, ch),
                device_id_type=MESH,
            ).start()

        for dy, dz, core in order(staged):
            send(dy, dz, core)
        send(0, 0, 1 - my_core)
        target[me] = source[me]

    def settle(source, target, slot):
        others = pl.ds(0, blocks - 1)
        copy = pltpu.make_async_copy(source.at[others], target.at[others], recv_sem.at[slot])
        copy.wait()

    def sent(source, target, slot):
        others = pl.ds(0, blocks - 1)
        copy = pltpu.make_async_copy(source.at[others], target.at[others], send_sem.at[slot])
        copy.wait()

    for g in range(GROUPS):
        spread(filt_out.at[g], filt_in.at[g], g, STAGED[0])
        if g == 0:
            edge.wait()
            for load in loads[2:4]:
                load.wait()
            for kind in range(3):
                ext[kind, 6:8, :] = jnp.where(me == 0, 0.0, edge_in[2 * kind : 2 * kind + 2, :])
        for j in range(half // rows):
            lanes = slice(g * half + j * rows, g * half + (j + 1) * rows)
            kinds = [
                taps[0, kind : kind + 1, lanes] * ext[kind, 8 : 8 + rows, lanes]
                + taps[1, kind : kind + 1, lanes] * ext[kind, 7 : 7 + rows, lanes]
                + taps[2, kind : kind + 1, lanes] * ext[kind, 6 : 6 + rows, lanes]
                for kind in range(3)
            ]
            product = kinds[1] * kinds[2]
            query[:, lanes] = kinds[0]
            direct[:, lanes] = skip[:, lanes] * product
            block = product.T.reshape(count, each, rows)
            prod_out[g, j * count : (j + 1) * count] = block.astype(BF16)
        spread(prod_out.at[g], prod_in.at[g], GROUPS + g, STAGED[1])
    for load in loads[4:]:
        load.wait()

    def forward(number):
        for c in range(0, number, 2):
            pair = jnp.concatenate(
                [stage[pl.ds(c + h, blocks, stride=number), :] for h in range(2)], 1
            ).astype(BF16)
            mixed = dot(outer[...], jnp.concatenate([pair, pair], 0))
            for h in range(2):
                lanes = slice(h * rows, (h + 1) * rows)
                real, imag = mixed[:blocks, lanes], mixed[blocks:, lanes]
                keep(
                    (c + h) * blocks,
                    jnp.concatenate(
                        [real * turn[0] + imag * turn[1], imag * turn[0] - real * turn[1]], 1
                    ),
                )

    def keep(start, value):
        high, low = split(value)
        pieces[start : start + blocks, : 2 * rows] = high
        pieces[start : start + blocks, 2 * rows : 4 * rows] = low
        pieces[start : start + blocks, 4 * rows :] = high

    for g in range(GROUPS):
        settle(filt_out.at[g], filt_in.at[g], g)
        stage[...] = filt_in[g].astype(F32).reshape(half, rows)
        forward(each)
        spectrum[...] = dot_split(pieces[...], fwd)
        settle(prod_out.at[g], prod_in.at[g], GROUPS + g)
        stage[...] = prod_in[g].astype(F32).reshape(half, rows)
        forward(each)
        signal[...] = dot_split(pieces[...], fwd)
        for start in range(0, half, blocks):
            here = slice(start, start + blocks)
            sig_re, sig_im = signal[here, :rows], signal[here, rows:]
            ans_re, ans_im = spectrum[here, :rows], spectrum[here, rows:]
            keep(
                start,
                jnp.concatenate(
                    [sig_re * ans_re - sig_im * ans_im, sig_re * ans_im + sig_im * ans_re], 1
                ),
            )
        signal[...] = dot_split(pieces[...], inv)
        for c in range(0, each, 2):
            turned = []
            for h in range(2):
                here = slice((c + h) * blocks, (c + h + 1) * blocks)
                real, imag = signal[here, :rows], signal[here, rows:]
                turned.append(
                    jnp.concatenate(
                        [real * turn[0] - imag * turn[1], imag * turn[0] + real * turn[1]], 0
                    )
                )
            high, low = split(jnp.concatenate(turned, 1))
            result = dot(
                jnp.concatenate([back[0], back[0], back[1]], 1),
                jnp.concatenate([high, low, high], 0),
            )
            for h in range(2):
                stage[pl.ds(c + h, blocks, stride=each), :] = result[
                    :, h * rows : (h + 1) * rows
                ]
        conv_out[g] = stage[...].reshape(blocks, each, rows).astype(BF16)
        spread(conv_out.at[g], conv_in.at[g], 2 * GROUPS + g, STAGED[2])

    fine = part.shape[3]
    wide = PARTS * fine
    right, left = lax.rem(ch + 1, 4), lax.rem(ch + 3, 4)
    far = lax.rem(ch + 2, 4)
    plan = [(far, 0), (far, 1), (right, 1), (left, 0), (right, 0), (left, 1), (ch, 0), (ch, 1)]

    def pass_on(slot, n):
        copy = pltpu.make_async_remote_copy(
            part.at[slot, n],
            part_in.at[slot, n],
            part_send.at[slot, n],
            part_recv.at[slot, n],
            device_id=(me, left if slot % 2 else right),
            device_id_type=MESH,
        )
        copy.start()
        return copy

    def project(g, slot, first=0, columns=wide):
        owner, side = plan[slot]
        start = pl.multiple_of(owner * 2 * wide + side * wide + first, 128)
        return dot(
            gated[:, g * half : (g + 1) * half],
            weight[g * half : (g + 1) * half, pl.ds(start, columns)],
        )

    copies = {}
    for g in range(GROUPS):
        settle(conv_out.at[g], conv_in.at[g], 2 * GROUPS + g)
        for j in range(half // rows):
            lanes = slice(g * half + j * rows, g * half + (j + 1) * rows)
            block = conv_in[g, j * count : (j + 1) * count].astype(F32).reshape(rows, rows)
            gated[:, lanes] = (query[:, lanes] * (block.T + direct[:, lanes])).astype(BF16)

        if g == GROUPS - 1:
            for slots in ((0, 1), (2, 3)):
                for n in range(PARTS):
                    for slot in slots:
                        piece = project(g, slot, n * fine, fine)
                        piece = piece + total[slot, :, n * fine : (n + 1) * fine]
                        part[slot, n] = piece.astype(BF16)
                        copies[slot, n] = pass_on(slot, n)
        for slot in range(0 if g < GROUPS - 1 else 4, 8):
            piece = project(g, slot) if g == 0 else total[slot] + project(g, slot)
            total[slot] = piece
    for n in range(PARTS):
        for slot in (4, 5):
            copies[slot - 4, n].wait()
            piece = total[slot, :, n * fine : (n + 1) * fine]
            part[slot, n] = (piece + part_in[slot - 4, n].astype(F32)).astype(BF16)
            copies[slot, n] = pass_on(slot, n)
    for g in range(GROUPS):
        sent(filt_out.at[g], filt_in.at[g], g)
        sent(prod_out.at[g], prod_in.at[g], GROUPS + g)
        sent(conv_out.at[g], conv_in.at[g], 2 * GROUPS + g)
    for slot in (2, 3):
        for n in range(PARTS):
            copies[slot, n].wait()
    for n in range(PARTS):
        for side, slots in enumerate([(3, 4), (2, 5)]):
            copies[4 + side, n].wait()
        for side, slots in enumerate([(3, 4), (2, 5)]):
            piece = total[6 + side, :, n * fine : (n + 1) * fine]
            for slot in slots:
                piece = piece + part_in[slot, n].astype(F32)
            out_ref[:, side * wide + n * fine : side * wide + (n + 1) * fine] = piece.astype(BF16)


def local(features, short_weights, long_filter, skip_gain, out_weight):
    rows, _, chans = features.shape
    blocks, groups = lax.axis_size("seq"), lax.axis_size("ch")
    width = out_weight.shape[1] // groups
    consts = tables(blocks, rows)
    operands = (
        jnp.transpose(features, (1, 0, 2)),
        short_weights,
        long_filter,
        skip_gain.reshape(1, chans),
        out_weight,
        *consts,
    )
    vmem = pltpu.VMEM
    return pl.pallas_call(
        functools.partial(kernel, (blocks, groups, rows, chans)),
        out_shape=pltpu.VMEM((rows, width), BF16),
        in_specs=[pl.BlockSpec(memory_space=pl.ANY)] * len(operands),
        out_specs=pl.BlockSpec(memory_space=pltpu.VMEM),
        scratch_shapes=[
            *[vmem(x.shape, x.dtype) for x in operands],
            vmem((3, rows + 8, chans), F32),
            vmem((8, chans), F32),
            vmem((8, chans), F32),
            vmem((rows, chans), F32),
            vmem((rows, chans), F32),
            *[vmem((GROUPS, blocks, chans // blocks // GROUPS, rows), BF16)] * 6,
            vmem((chans // GROUPS, rows), F32),
            vmem((chans // GROUPS, 2 * rows), F32),
            vmem((chans // GROUPS, 2 * rows), F32),
            vmem((chans // GROUPS, 6 * rows), BF16),
            vmem((8, rows, width // 2), F32),
            vmem((rows, chans), BF16),
            vmem((6, PARTS, rows, width // 2 // PARTS), BF16),
            vmem((6, PARTS, rows, width // 2 // PARTS), BF16),
            pltpu.SemaphoreType.DMA((len(operands),)),
            pltpu.SemaphoreType.DMA((2,)),
            pltpu.SemaphoreType.DMA((3 * GROUPS,)),
            pltpu.SemaphoreType.DMA((3 * GROUPS,)),
            pltpu.SemaphoreType.DMA((6, PARTS)),
            pltpu.SemaphoreType.DMA((6, PARTS)),
        ],
        compiler_params=pltpu.CompilerParams(
            collective_id=0, has_side_effects=True, vmem_limit_bytes=62 * 2**20
        ),
        name="convolve_project",
    )(*operands)


def solution(mesh):
    in_specs = (P("seq", None, "ch"), P(None, None, "ch"), P("seq", "ch"), P("ch"), P("ch", None))
    out_specs = P("seq", "ch")
    return jax.shard_map(local, mesh=mesh, in_specs=in_specs, out_specs=out_specs, check_vma=False)
```
